32 devices in a mesh: view: 2 (over x), expert: 4 (over z), col: 4 (over y, core).
Axes of the slice: x: 2, y: 2, z: 4, core: 2. Of those that a mesh axis runs over, the one named last changes fastest.
Arguments:
- tokens: bfloat16 [4096, 2560], P(('view', 'expert', 'col')), may hold values from -6 to 6
- expert_ids: int32 [4096, 2], P(('view', 'expert', 'col')), may hold values from 0 to 3, all different within a row; in each aligned block of 128 rows (0 to 127, 128 to 255, ...) at most 68 rows name the same one
- gate_codes: int32 [4096, 2], P(('view', 'expert', 'col')), may hold values from 1 to 1023
- fake_score: bfloat16 [4096, 2560], P(('view', 'expert', 'col')), may hold values from -6 to 6
- gate_weight: bfloat16 [4, 2560, 3456], P('expert', 'view', 'col'), may hold values from -0.125 to 0.125
- up_weight: bfloat16 [4, 2560, 3456], P('expert', 'view', 'col'), may hold values from -0.125 to 0.125
- down_weight: bfloat16 [4, 3456, 2560], P('expert', 'col', 'view'), may hold values from -0.109375 to 0.109375
Outputs:
- score_gap: bfloat16 [4096, 2560], P(('view', 'expert', 'col'))
The draws below stay inside these ranges and needn't reach their ends.
Inputs may be any that keep to these rules, and one draw needn't show every extreme that they name: `expert_ids`: each row names two different experts; within the 128 rows of one device no expert is named by more than 68 rows, a bound that some block reaches.
All inputs are finite; a program needn't handle non-finite values.
Results may differ from the reference program's by a relative error of at most 0.007.
Values may be sent and summed in bfloat16 or wider, within the bound.
A program may use at most 128 MiB of HBM per device.

```python
import math
import jax
import jax.numpy as jnp
import numpy as np
from jax import lax

D = 2560
FF = 3456
NE = 4
TOK_DEV = 128
CAP = 68
TOKENS = 4096
N_COL = 4


def with_ends(entries, stream_key, smallest, largest):
    spot = [jax.random.randint(jax.random.fold_in(stream_key, axis), (), 0, length) for axis, length in enumerate(entries.shape)]
    widest = entries.shape.index(max(entries.shape))
    next_to = spot[:widest] + [(spot[widest] + 1) % entries.shape[widest]] + spot[widest + 1:]
    return entries.at[tuple(spot)].set(smallest).at[tuple(next_to)].set(largest)


def block_levels(rng, shape, pieces, least, largest):
    loudness = 1.0
    for axis_at, parts in pieces:
        heights = jax.random.uniform(jax.random.fold_in(jax.random.fold_in(rng, 6), axis_at), (parts,), jnp.float32, least / len(pieces), largest / len(pieces))
        loudness = loudness * jnp.repeat(jnp.exp(heights), shape[axis_at] // parts).reshape((-1,) + (1,) * (len(shape) - 1 - axis_at))
    return loudness


def deal_out(key, own, number, rows, number_of, top, most, lean):
    ranking = jax.random.permutation(key, number_of)
    heavy_load, common = portions_of(number_of, rows * top, most, lean, True), portions_of(number_of, rows * top, most, lean, False)
    places = jnp.arange(number_of)

    def named(sizes, offset_by):
        used = int((sizes > 0).sum())
        fixed = max(1, used // 4)
        shifted = fixed + (places - fixed + offset_by * (used - fixed)) % max(1, number_of - fixed)
        return jnp.zeros((number_of,), jnp.int32).at[ranking[jnp.where(places < fixed, places, shifted)]].set(jnp.asarray(sizes, jnp.int32))

    sizes = jnp.where(number % 4 == 0, named(heavy_load, number // 4), named(common, number - number // 4 - 1))
    mixed = jax.random.permutation(jax.random.fold_in(own, 3), number_of)
    source_of, taker = mixed[0:number_of // 2 * 2:2], mixed[1:number_of // 2 * 2:2]
    slack = jnp.minimum(sizes[source_of] - 1, most - sizes[taker]) // 2
    slack = jnp.where((source_of == ranking[0]) | (taker == ranking[0]) | (sizes[taker] == 0), 0, jnp.maximum(slack, 0))
    shifted = jax.random.randint(jax.random.fold_in(own, 4), (number_of // 2,), 0, 1 << 20) % (slack + 1)
    sizes = sizes.at[source_of].add(-shifted).at[taker].add(shifted)
    labels = jnp.searchsorted(jnp.cumsum(sizes), jnp.arange(rows * top), side="right").astype(jnp.int32)
    table = labels.reshape(top, rows).T
    table = table[jax.random.permutation(jax.random.fold_in(own, 1), rows)]
    offset_by = jax.random.randint(jax.random.fold_in(own, 2), (rows, 1), 0, top)
    return jnp.take_along_axis(table, (jnp.arange(top)[None, :] + offset_by) % top, axis=1)


def portions_of(count, total, limit, lean, full):
    loads = [(1 << 20) // math.isqrt(grade ** lean) + 1 for grade in range(1, count + 1)]
    largest = limit if full else min(limit, max(-(-total // count), total * loads[0] // sum(loads)))
    least = 1 if total - largest >= count - 1 else 0
    counts, surplus = [largest] + [least] * (count - 1), total - largest - least * (count - 1)
    while surplus > 0:
        movable = [i for i in range(1, count) if counts[i] < largest] or [i for i in range(1, count) if counts[i] < limit]
        mass, left = sum([loads[i] for i in movable]), surplus
        for i in movable:
            extra = min(limit - counts[i], max(1, left * loads[i] // mass), surplus)
            counts[i] = counts[i] + extra
            surplus = surplus - extra
    return np.array(counts)


def gaussian(own_key, dims, scale, most, pieces=(), kind=jnp.bfloat16):
    gain = block_levels(own_key, dims, pieces, -0.22, 0.18) if pieces else 1.0
    values = jax.random.normal(own_key, dims, jnp.float32) * scale * gain
    return jnp.minimum(jnp.maximum(values, -most), most).astype(kind)


def setup_inputs(seed: int = 0) -> dict:
    arg_keys = jax.random.split(jax.random.key(seed), 8)
    tokens = gaussian(arg_keys[0], (TOKENS, D), 1.0, 6.0, ((0, 32),))
    expert_ids_keys = jax.random.split(jax.random.fold_in(arg_keys[1], 1), TOKENS // TOK_DEV)
    expert_ids_turns = jax.random.permutation(jax.random.fold_in(arg_keys[1], 3), TOKENS // TOK_DEV)
    expert_ids = jax.vmap(lambda own, number: deal_out(jax.random.fold_in(arg_keys[1], 2), own, number, TOK_DEV, NE, 2, CAP, 2))(expert_ids_keys, expert_ids_turns).reshape((TOKENS, 2))
    gate_codes = with_ends(jax.random.randint(arg_keys[2], (TOKENS, 2), 1, 1024), jax.random.fold_in(arg_keys[2], 1), 1, 1023).astype(jnp.int32)
    fake_score = gaussian(arg_keys[3], (TOKENS, D), 1.0, 6.0, ((0, 32),))
    gate_weight = gaussian(arg_keys[4], (NE, D, FF), D ** -0.5, 0.125, ((0, 4), (1, 2), (2, 4)))
    up_weight = gaussian(arg_keys[5], (NE, D, FF), D ** -0.5, 0.125, ((0, 4), (1, 2), (2, 4)))
    down_weight = gaussian(arg_keys[6], (NE, FF, D), FF ** -0.5, 0.109375, ((0, 4), (1, 4), (2, 2)))
    return {"tokens": tokens, "expert_ids": expert_ids, "gate_codes": gate_codes, "fake_score": fake_score, "gate_weight": gate_weight, "up_weight": up_weight, "down_weight": down_weight}


def expert_rows(buffer, w_gate, w_up, w_down):
    gate = jnp.dot(buffer, w_gate, preferred_element_type=jnp.float32)
    up = jnp.dot(buffer, w_up, preferred_element_type=jnp.float32)
    hidden = (jax.nn.silu(gate) * up).astype(jnp.bfloat16)
    width = FF // N_COL
    total = jnp.zeros((buffer.shape[0], D), jnp.float32)
    for piece in range(N_COL):
        part = jnp.dot(hidden[:, piece * width:(piece + 1) * width], w_down[piece * width:(piece + 1) * width], preferred_element_type=jnp.float32).astype(jnp.bfloat16)
        part = lax.optimization_barrier(part)
        total = total + part.astype(jnp.float32)
    return total.astype(jnp.bfloat16)


def reference(tokens, expert_ids, gate_codes, fake_score, gate_weight, up_weight, down_weight):
    blocks = TOKENS // TOK_DEV
    ids = expert_ids.reshape(blocks, TOK_DEV, 2)
    codes = gate_codes.reshape(blocks, TOK_DEV, 2)
    hits = ids[:, :, :, None] == jnp.arange(NE).astype(jnp.int32)[None, None, None, :]
    routed = jnp.sum(hits.astype(jnp.int32), axis=2)
    before = jnp.cumsum(routed, axis=1) - routed
    slot = jnp.sum(jnp.where(hits, before[:, :, None, :], 0), axis=3)
    base = (jnp.arange(blocks).astype(jnp.int32) * CAP)[:, None]
    teacher = jnp.zeros((TOKENS, D), jnp.float32)
    for expert in range(NE):
        mark = ids == expert
        chosen = jnp.any(mark, axis=2)
        where_slot = jnp.sum(jnp.where(mark, slot, 0), axis=2)
        target = jnp.where(chosen, base + where_slot, blocks * CAP).reshape(-1)
        buffer = jnp.zeros((blocks * CAP, D), jnp.bfloat16).at[target].set(tokens, mode="drop")
        result = expert_rows(buffer, gate_weight[expert], up_weight[expert], down_weight[expert])
        picked = result[jnp.minimum(target, blocks * CAP - 1)].astype(jnp.float32)
        weight = jnp.sum(jnp.where(mark, codes, 0), axis=2).astype(jnp.float32).reshape(-1) / 1024.0
        teacher = teacher + weight[:, None] * picked
    return (fake_score.astype(jnp.float32) - teacher).astype(jnp.bfloat16)
```

```python
import jax
import jax.numpy as jnp
from jax import lax
from jax.sharding import PartitionSpec as P

D = 2560
NE = 4
CAP = 68


def on_device(tokens, expert_ids, gate_codes, fake_score, gate_weight, up_weight, down_weight):
    slots_all = NE * CAP
    hits = expert_ids[:, :, None] == jnp.arange(NE)[None, None, :]
    routed = jnp.sum(hits.astype(jnp.int32), axis=1)
    before = jnp.cumsum(routed, axis=0) - routed
    slot = jnp.sum(jnp.where(hits, before[:, None, :], 0), axis=2)
    target = expert_ids * CAP + slot
    place = target[:, :, None] == jnp.arange(slots_all)[None, None, :]
    select = jnp.any(place, axis=1).astype(jnp.bfloat16)
    outgoing = jnp.dot(select.T, tokens, preferred_element_type=jnp.float32).astype(jnp.bfloat16)
    v = lax.axis_index("view")
    half = gate_weight.shape[1]
    swap = [(0, 1), (1, 0)]
    other = [lax.ppermute(w[0], "view", swap) for w in (gate_weight, up_weight, down_weight)]
    arrived = lax.all_to_all(
        outgoing.reshape(NE, CAP, D), "expert", split_axis=0, concat_axis=0, tiled=True
    )
    gathered = lax.all_gather(arrived, "col", axis=0, tiled=True)
    inputs = gathered.reshape(-1, D)
    mine = lax.dynamic_slice_in_dim(inputs, v * half, half, axis=1)
    theirs = lax.dynamic_slice_in_dim(inputs, (1 - v) * half, half, axis=1)

    def project(own, far):
        return jnp.dot(mine, own, preferred_element_type=jnp.float32) + jnp.dot(
            theirs, far, preferred_element_type=jnp.float32
        )

    gate = project(gate_weight[0], other[0])
    up = project(up_weight[0], other[1])
    hidden = (jax.nn.silu(gate) * up).astype(jnp.bfloat16)
    near = jnp.dot(hidden, down_weight[0], preferred_element_type=jnp.float32)
    far = jnp.dot(hidden, other[2], preferred_element_type=jnp.float32)
    near, far = near.astype(jnp.bfloat16), far.astype(jnp.bfloat16)
    partial_out = jnp.concatenate(
        [jnp.where(v == 0, near, far), jnp.where(v == 0, far, near)], axis=1
    )
    summed = lax.psum_scatter(
        partial_out, "col", scatter_dimension=0, tiled=True
    )
    back = lax.all_to_all(
        summed.reshape(NE, CAP, D), "expert", split_axis=0, concat_axis=0, tiled=True
    )
    results = back.reshape(slots_all, D)
    weights = gate_codes.astype(jnp.float32) / 1024.0
    teacher = jnp.zeros((tokens.shape[0], D), jnp.float32)
    for route in range(2):
        picker = place[:, route, :].astype(jnp.bfloat16)
        picked = jnp.dot(picker, results, preferred_element_type=jnp.float32)
        teacher = teacher + weights[:, route][:, None] * picked
    return (fake_score.astype(jnp.float32) - teacher).astype(jnp.bfloat16)


def on_device_general(tokens, expert_ids, gate_codes, fake_score, gate_weight, up_weight, down_weight):
    slots_all = NE * CAP
    hits = expert_ids[:, :, None] == jnp.arange(NE)[None, None, :]
    routed = jnp.sum(hits.astype(jnp.int32), axis=1)
    before = jnp.cumsum(routed, axis=0) - routed
    slot = jnp.sum(jnp.where(hits, before[:, None, :], 0), axis=2)
    target = expert_ids * CAP + slot
    place = target[:, :, None] == jnp.arange(slots_all)[None, None, :]
    select = jnp.any(place, axis=1).astype(jnp.bfloat16)
    outgoing = jnp.dot(select.T, tokens, preferred_element_type=jnp.float32).astype(jnp.bfloat16)
    arrived = lax.all_to_all(
        outgoing.reshape(NE, CAP, D), "expert", split_axis=0, concat_axis=0, tiled=True
    )
    gathered = lax.all_gather(arrived, "col", axis=0, tiled=True)
    inputs = gathered.reshape(-1, D)

    def add_rows(piece):
        return jnp.dot(inputs, piece[0], preferred_element_type=jnp.float32)

    gate = add_rows(lax.all_gather(gate_weight, "view", axis=1, tiled=True))
    up = add_rows(lax.all_gather(up_weight, "view", axis=1, tiled=True))
    hidden = (jax.nn.silu(gate) * up).astype(jnp.bfloat16)
    partial_out = jnp.dot(
        hidden,
        lax.all_gather(down_weight, "view", axis=2, tiled=True)[0],
        preferred_element_type=jnp.float32,
    ).astype(jnp.bfloat16)
    partial_out = lax.optimization_barrier(partial_out).astype(jnp.float32)
    summed = lax.psum_scatter(
        partial_out.astype(jnp.bfloat16), "col", scatter_dimension=0, tiled=True
    )
    back = lax.all_to_all(
        summed.reshape(NE, CAP, D), "expert", split_axis=0, concat_axis=0, tiled=True
    )
    results = back.reshape(slots_all, D)
    weights = gate_codes.astype(jnp.float32) / 1024.0
    teacher = jnp.zeros((tokens.shape[0], D), jnp.float32)
    for route in range(2):
        picker = place[:, route, :].astype(jnp.bfloat16)
        picked = jnp.dot(picker, results, preferred_element_type=jnp.float32)
        teacher = teacher + weights[:, route][:, None] * picked
    return (fake_score.astype(jnp.float32) - teacher).astype(jnp.bfloat16)


def solution(mesh):
    in_specs = (
        P(("view", "expert", "col"), None),
        P(("view", "expert", "col"), None),
        P(("view", "expert", "col"), None),
        P(("view", "expert", "col"), None),
        P("expert", "view", "col"),
        P("expert", "view", "col"),
        P("expert", "col", "view"),
    )
    out_specs = P(("view", "expert", "col"), None)
    return jax.shard_map(
        on_device if mesh.shape["view"] == 2 else on_device_general, mesh=mesh, in_specs=in_specs, out_specs=out_specs, check_vma=False
    )
```

```python
import functools

import jax
import jax.numpy as jnp
from jax import lax
from jax.experimental import pallas as pl
from jax.experimental.pallas import tpu as pltpu
from jax.sharding import PartitionSpec as P

D = 2560
NE = 4
CAP = 68
PAIR = 144
F32 = jnp.float32
BF16 = jnp.bfloat16
NEAR = (((1,), (1,)), ((), ()))


def fused(ids_ref, codes_ref, tok_ref, fake_ref, wg_ref, wu_ref, wd_ref, out_ref,
          near_g, near_u, far_g, far_u, down, x, sent_z, gate, up, hidden,
          place, sib_place, sib_tok, sib_fake, combine,
          part, core_in, pair_sum, y_in, y_sum, back, sib_gap, gap_in,
          far_send, far_recv, down_send, down_recv, near_sem, near_down,
          sib_send, sib_recv, z_send, z_recv, y_send, y_recv, c_send, c_recv,
          a_send, a_recv, b_send, b_recv, e_send, e_recv, g_send, g_recv):
    v, e, c = lax.axis_index("view"), lax.axis_index("expert"), lax.axis_index("col")
    k, y = c % 2, c // 2
    half = D // 2
    chunks = down.shape[0]
    per_view = chunks // 2
    wide = down.shape[2]
    lane = wide // 2
    tokens = tok_ref.shape[0]
    blocks = gate.shape[0]
    rows = gate.shape[1]
    ff = gate.shape[2]
    to_view = (1 - v, e, c)
    to_sib = (v, e, y * 2 + 1 - k)
    to_y = (v, e, (1 - y) * 2 + k)

    def remote(src, dst, send, recv, device):
        return pltpu.make_async_remote_copy(
            src_ref=src, dst_ref=dst, send_sem=send, recv_sem=recv,
            device_id=device, device_id_type=pl.DeviceIdType.MESH)

    def expert_at(step):
        return (e + step) % NE

    barrier = pltpu.get_barrier_semaphore()
    others = [to_view, to_sib, to_y] + [(v, expert_at(s), c) for s in range(1, NE)]
    for device in others:
        pl.semaphore_signal(barrier, inc=1, device_id=device, device_id_type=pl.DeviceIdType.MESH)
    pl.semaphore_wait(barrier, len(others))

    send_g = remote(wg_ref, far_g, far_send.at[0], far_recv.at[0], to_view)
    send_u = remote(wu_ref, far_u, far_send.at[1], far_recv.at[1], to_view)
    send_g.start()
    send_u.start()
    send_tok = remote(tok_ref.at[:, pl.ds(pl.multiple_of((1 - k) * half, half), half)], sib_tok,
                      sib_send.at[0], sib_recv.at[0], to_sib)
    send_tok.start()
    send_fake = remote(fake_ref, sib_fake, sib_send.at[1], sib_recv.at[1], to_sib)
    send_fake.start()
    own_g = pltpu.make_async_copy(wg_ref, near_g, near_sem.at[0])
    own_u = pltpu.make_async_copy(wu_ref, near_u, near_sem.at[1])
    own_g.start()
    own_u.start()

    def own_down(j):
        return pltpu.make_async_copy(
            wd_ref.at[:, pl.ds(pl.multiple_of(j * wide, wide), wide)], down.at[j], near_down.at[j])

    def far_down(j):
        return remote(wd_ref.at[:, pl.ds(pl.multiple_of(j * wide, wide), wide)],
                      down.at[per_view + j], down_send.at[j], down_recv.at[j], to_view)

    for j in range(per_view):
        own_down(j).start()

    id0, id1 = ids_ref[0:1, :], ids_ref[1:2, :]
    which = lax.broadcasted_iota(jnp.int32, (16, tokens), 0)
    hits = jnp.where((which == id0) | (which == id1), 1.0, 0.0).astype(BF16)
    earlier = jnp.where(
        lax.broadcasted_iota(jnp.int32, (tokens, tokens), 0)
        < lax.broadcasted_iota(jnp.int32, (tokens, tokens), 1), 1.0, 0.0).astype(BF16)
    before = jnp.dot(hits, earlier, preferred_element_type=F32)
    slot0 = jnp.sum(jnp.where(which == id0, before, 0.0), axis=0, keepdims=True).astype(jnp.int32)
    slot1 = jnp.sum(jnp.where(which == id1, before, 0.0), axis=0, keepdims=True).astype(jnp.int32)
    row = lax.broadcasted_iota(jnp.int32, (NE * PAIR, tokens), 0)
    is0 = row == id0 * PAIR + k * CAP + slot0
    is1 = row == id1 * PAIR + k * CAP + slot1
    code0, code1 = codes_ref[0:1, :], codes_ref[1:2, :]
    hi0, hi1 = (code0 // 32).astype(F32) / 32.0, (code1 // 32).astype(F32) / 32.0
    lo0, lo1 = (code0 % 32).astype(F32) / 1024.0, (code1 % 32).astype(F32) / 1024.0
    hi = jnp.where(is0, hi0, 0.0) + jnp.where(is1, hi1, 0.0)
    lo = jnp.where(is0, lo0, 0.0) + jnp.where(is1, lo1, 0.0)
    place[0] = hi.astype(BF16)
    place[1] = lo.astype(BF16)
    send_place = remote(place, sib_place, sib_send.at[2], sib_recv.at[2], to_sib)
    send_place.start()
    select = jnp.where(is0 | is1, 1.0, 0.0).astype(BF16)
    mine = jnp.dot(select, tok_ref[:, pl.ds(pl.multiple_of(k * half, half), half)],
                   preferred_element_type=F32)
    send_tok.wait_recv()
    send_place.wait_recv()
    sib_hi, sib_lo = sib_place[0].astype(F32), sib_place[1].astype(F32)
    sib_select = jnp.where(sib_hi + sib_lo > 0.0, 1.0, 0.0).astype(BF16)
    both = mine + jnp.dot(sib_select, sib_tok[...], preferred_element_type=F32)
    sent_z[...] = both.astype(BF16).reshape(NE, PAIR, half)
    x[k, y, e] = sent_z[e]

    def z_copy(s):
        peer = expert_at(s)
        return remote(sent_z.at[peer], x.at[k, y, e], z_send.at[s - 1], z_recv.at[s - 1], (v, peer, c))

    def z_arrived(s):
        return remote(sent_z.at[0], x.at[k, y, expert_at(NE - s)], z_send.at[s - 1], z_recv.at[s - 1], to_view)

    def y_copy(s):
        at = x.at[k, y, expert_at(NE - s)]
        return remote(at, at, y_send.at[s], y_recv.at[s], to_y)

    def y_arrived(s):
        at = x.at[k, 1 - y, expert_at(NE - s)]
        return remote(at, at, y_send.at[s], y_recv.at[s], to_y)

    def c_copy(s, far):
        at = x.at[k, (1 - y) if far else y, expert_at(NE - s)]
        return remote(at, at, c_send.at[far, s], c_recv.at[far, s], to_sib)

    def c_arrived(s, far):
        at = x.at[1 - k, (1 - y) if far else y, expert_at(NE - s)]
        return remote(at, at, c_send.at[far, s], c_recv.at[far, s], to_sib)

    for s in range(1, NE):
        z_copy(s).start()
    y_copy(0).start()
    c_copy(0, 0).start()
    combine[0, 0:tokens] = hi.T.astype(BF16)
    combine[1, 0:tokens] = lo.T.astype(BF16)
    combine[0, tokens:2 * tokens] = sib_hi.T.astype(BF16)
    combine[1, tokens:2 * tokens] = sib_lo.T.astype(BF16)
    for s in range(1, NE):
        z_arrived(s).wait_recv()
        y_copy(s).start()
        c_copy(s, 0).start()
    for s in range(NE):
        y_arrived(s).wait_recv()
        c_copy(s, 1).start()
    for far in range(2):
        for s in range(NE):
            c_arrived(s, far).wait_recv()

    def x_rows(view, i):
        return x[view, i // 2, pl.ds((i % 2) * 2, 2)].reshape(rows, half)

    own_g.wait()
    own_u.wait()

    @pl.loop(0, blocks)
    def _(i):
        gate[i] = lax.dot_general(x_rows(v, i), near_g[...], NEAR, preferred_element_type=F32)
        up[i] = lax.dot_general(x_rows(v, i), near_u[...], NEAR, preferred_element_type=F32)

    send_g.wait_recv()

    @pl.loop(0, blocks)
    def _(i):
        gate[i] += lax.dot_general(x_rows(1 - v, i), far_g[...], NEAR, preferred_element_type=F32)

    send_u.wait_recv()
    far_down(0).start()
    far_down(1).start()

    @pl.loop(0, blocks)
    def _(i):
        u = up[i] + lax.dot_general(x_rows(1 - v, i), far_u[...], NEAR, preferred_element_type=F32)
        g = gate[i]
        hidden[i] = (g / (1.0 + jnp.exp(-g)) * u).astype(BF16)

    def stage_a(j):
        return remote(part.at[j, 1 - k], core_in.at[j], a_send.at[j], a_recv.at[j], to_sib)

    def stage_b(j):
        return remote(pair_sum.at[j, 1 - y], y_in.at[j], b_send.at[j], b_recv.at[j], to_y)

    def stage_c(j, s):
        peer = expert_at(s)
        return remote(y_sum.at[j, peer], back.at[j, e], e_send.at[s - 1, j], e_recv.at[s - 1, j], (v, peer, c))

    def stage_c_in(j, s):
        return remote(y_sum.at[j, 0], back.at[j, expert_at(NE - s)], e_send.at[s - 1, j], e_recv.at[s - 1, j], to_view)

    def stage_d(j):
        return remote(sib_gap.at[j], gap_in.at[j], g_send.at[j], g_recv.at[j], to_sib)

    def columns(j, core):
        first = (j // per_view + v) % 2 * half + (j % per_view) * wide + core * lane
        return pl.ds(pl.multiple_of(first, lane), lane)

    send_fake.wait_recv()

    @pl.loop(0, chunks + 3)
    def _(t):
        @pl.when(t < per_view)
        def _():
            own_down(t).wait()

        @pl.when((t >= per_view) & (t < chunks))
        def _():
            far_down(t - per_view).wait_recv()

        @pl.when((t >= per_view) & (t < chunks - 2))
        def _():
            far_down(t - per_view + 2).start()

        @pl.when(t < chunks)
        def _():
            @pl.loop(0, blocks)
            def _(i):
                p = jnp.dot(hidden[i], down[t], preferred_element_type=F32).astype(BF16)
                at = pl.ds(pl.multiple_of(i * rows, rows), rows)
                part[t, 0, at, :] = p[:, :lane]
                part[t, 1, at, :] = p[:, lane:]
            stage_a(t).start()

        @pl.when((t >= 1) & (t < chunks + 1))
        def _():
            j = t - 1
            stage_a(j).wait_recv()
            total = part[j, k].astype(F32) + core_in[j].astype(F32)
            pair_sum[j] = total.astype(BF16).reshape(2, NE * PAIR, lane)
            stage_b(j).start()

        @pl.when((t >= 2) & (t < chunks + 2))
        def _():
            j = t - 2
            stage_b(j).wait_recv()
            total = pair_sum[j, y].astype(F32) + y_in[j].astype(F32)
            y_sum[j] = total.astype(BF16).reshape(NE, PAIR, lane)
            for s in range(1, NE):
                stage_c(j, s).start()
            back[j, e] = y_sum[j, e]

        @pl.when(t >= 3)
        def _():
            j = t - 3
            for s in range(1, NE):
                stage_c_in(j, s).wait_recv()
            result = back[j].reshape(NE * PAIR, lane)
            teacher = jnp.dot(combine[0], result, preferred_element_type=F32) + jnp.dot(
                combine[1], result, preferred_element_type=F32)
            at = columns(j, k)
            sib_gap[j] = (sib_fake[:, at].astype(F32) - teacher[tokens:]).astype(BF16)
            stage_d(j).start()
            out_ref[:, at] = (fake_ref[:, at].astype(F32) - teacher[:tokens]).astype(BF16)

    @pl.loop(0, chunks)
    def _(j):
        stage_d(j).wait_recv()
        out_ref[:, columns(j, 1 - k)] = gap_in[j]
        stage_a(j).wait_send()
        stage_b(j).wait_send()
        for s in range(1, NE):
            stage_c(j, s).wait_send()
        stage_d(j).wait_send()

    for j in range(per_view):
        far_down(j).wait_send()
    for copy in (send_g, send_u, send_tok, send_fake, send_place):
        copy.wait_send()
    for s in range(1, NE):
        z_copy(s).wait_send()
    for s in range(NE):
        y_copy(s).wait_send()
        c_copy(s, 0).wait_send()
        c_copy(s, 1).wait_send()


def on_device_fused(tokens, expert_ids, gate_codes, fake_score, gate_weight, up_weight, down_weight):
    ff, half = gate_weight.shape[2], gate_weight.shape[1]
    count = tokens.shape[0]
    chunks, wide, lane = 10, 256, 128
    total = 8 * PAIR
    dma = pltpu.SemaphoreType.DMA
    vmem = pl.BlockSpec(memory_space=pltpu.VMEM)
    anywhere = pl.BlockSpec(memory_space=pl.ANY)
    return pl.pallas_call(
        fused,
        out_shape=jax.ShapeDtypeStruct((count, D), BF16),
        in_specs=[vmem] * 4 + [anywhere] * 3,
        out_specs=vmem,
        scratch_shapes=[
            pltpu.VMEM((ff, half), BF16), pltpu.VMEM((ff, half), BF16),
            pltpu.VMEM((ff, half), BF16), pltpu.VMEM((ff, half), BF16),
            pltpu.VMEM((chunks, ff, wide), BF16),
            pltpu.VMEM((2, 2, NE, PAIR, half), BF16),
            pltpu.VMEM((NE, PAIR, half), BF16),
            pltpu.VMEM((4, total // 4, ff), F32), pltpu.VMEM((4, total // 4, ff), F32),
            pltpu.VMEM((4, total // 4, ff), BF16),
            pltpu.VMEM((2, NE * PAIR, count), BF16), pltpu.VMEM((2, NE * PAIR, count), BF16),
            pltpu.VMEM((count, half), BF16), pltpu.VMEM((count, D), BF16),
            pltpu.VMEM((2, 2 * count, NE * PAIR), BF16),
            pltpu.VMEM((chunks, 2, total, lane), BF16),
            pltpu.VMEM((chunks, total, lane), BF16),
            pltpu.VMEM((chunks, 2, NE * PAIR, lane), BF16),
            pltpu.VMEM((chunks, NE * PAIR, lane), BF16),
            pltpu.VMEM((chunks, NE, PAIR, lane), BF16),
            pltpu.VMEM((chunks, NE, PAIR, lane), BF16),
            pltpu.VMEM((chunks, count, lane), BF16), pltpu.VMEM((chunks, count, lane), BF16),
            dma((2,)), dma((2,)), dma((chunks // 2,)), dma((chunks // 2,)), dma((2,)), dma((chunks // 2,)),
            dma((3,)), dma((3,)), dma((NE - 1,)), dma((NE - 1,)), dma((NE,)), dma((NE,)),
            dma((2, NE)), dma((2, NE)),
            dma((chunks,)), dma((chunks,)), dma((chunks,)), dma((chunks,)),
            dma((NE - 1, chunks)), dma((NE - 1, chunks)), dma((chunks,)), dma((chunks,)),
        ],
        compiler_params=pltpu.CompilerParams(
            collective_id=0, has_side_effects=True, vmem_limit_bytes=60 * 1024 * 1024),
        cost_estimate=pl.CostEstimate(
            flops=6 * total * D * ff, bytes_accessed=6 * D * ff, transcendentals=total * ff),
    )(
        expert_ids.T, gate_codes.T, tokens, fake_score,
        gate_weight[0].T, up_weight[0].T, down_weight[0],
    )


def on_device(tokens, expert_ids, gate_codes, fake_score, gate_weight, up_weight, down_weight):
    slots_all = NE * CAP
    hits = expert_ids[:, :, None] == jnp.arange(NE)[None, None, :]
    routed = jnp.sum(hits.astype(jnp.int32), axis=1)
    before = jnp.cumsum(routed, axis=0) - routed
    slot = jnp.sum(jnp.where(hits, before[:, None, :], 0), axis=2)
    target = expert_ids * CAP + slot
    place = target[:, :, None] == jnp.arange(slots_all)[None, None, :]
    select = jnp.any(place, axis=1).astype(jnp.bfloat16)
    outgoing = jnp.dot(select.T, tokens, preferred_element_type=jnp.float32).astype(jnp.bfloat16)
    arrived = lax.all_to_all(
        outgoing.reshape(NE, CAP, D), "expert", split_axis=0, concat_axis=0, tiled=True
    )
    gathered = lax.all_gather(arrived, "col", axis=0, tiled=True)
    inputs = gathered.reshape(-1, D)

    def add_rows(piece):
        return jnp.dot(inputs, piece[0], preferred_element_type=jnp.float32)

    gate = add_rows(lax.all_gather(gate_weight, "view", axis=1, tiled=True))
    up = add_rows(lax.all_gather(up_weight, "view", axis=1, tiled=True))
    hidden = (jax.nn.silu(gate) * up).astype(jnp.bfloat16)
    partial_out = jnp.dot(
        hidden,
        lax.all_gather(down_weight, "view", axis=2, tiled=True)[0],
        preferred_element_type=jnp.float32,
    ).astype(jnp.bfloat16)
    partial_out = lax.optimization_barrier(partial_out).astype(jnp.float32)
    summed = lax.psum_scatter(
        partial_out.astype(jnp.bfloat16), "col", scatter_dimension=0, tiled=True
    )
    back = lax.all_to_all(
        summed.reshape(NE, CAP, D), "expert", split_axis=0, concat_axis=0, tiled=True
    )
    results = back.reshape(slots_all, D)
    weights = gate_codes.astype(jnp.float32) / 1024.0
    teacher = jnp.zeros((tokens.shape[0], D), jnp.float32)
    for route in range(2):
        picker = place[:, route, :].astype(jnp.bfloat16)
        picked = jnp.dot(picker, results, preferred_element_type=jnp.float32)
        teacher = teacher + weights[:, route][:, None] * picked
    return (fake_score.astype(jnp.float32) - teacher).astype(jnp.bfloat16)


def solution(mesh):
    in_specs = (
        P(("view", "expert", "col"), None),
        P(("view", "expert", "col"), None),
        P(("view", "expert", "col"), None),
        P(("view", "expert", "col"), None),
        P("expert", "view", "col"),
        P("expert", "view", "col"),
        P("expert", "col", "view"),
    )
    out_specs = P(("view", "expert", "col"), None)
    return jax.shard_map(
        on_device_fused if mesh.shape["view"] == 2 else on_device, mesh=mesh, in_specs=in_specs, out_specs=out_specs, check_vma=False
    )
```

```python
import functools

import jax
import jax.numpy as jnp
from jax import lax
from jax.experimental import pallas as pl
from jax.experimental.pallas import tpu as pltpu
from jax.sharding import PartitionSpec as P

D = 2560
NE = 4
CAP = 68
PAIR = 144
F32 = jnp.float32
BF16 = jnp.bfloat16
NEAR = (((1,), (1,)), ((), ()))


def fused(ids_ref, codes_ref, tok_ref, fake_ref, wg_ref, wu_ref, wd_ref, out_ref,
          near_g, near_u, far_g, far_u, down, x, sent_z, gate, up, hidden,
          place, sib_place, sib_tok, sib_fake, combine,
          part, core_in, pair_sum, y_in, y_sum, back, sib_gap, gap_in,
          far_send, far_recv, down_send, down_recv, near_sem, near_down,
          sib_send, sib_recv, z_send, z_recv, y_send, y_recv, c_send, c_recv,
          a_send, a_recv, b_send, b_recv, e_send, e_recv, g_send, g_recv):
    v, e, c = lax.axis_index("view"), lax.axis_index("expert"), lax.axis_index("col")
    k, y = c % 2, c // 2
    half = D // 2
    chunks = down.shape[0]
    per_view = chunks // 2
    wide = down.shape[2]
    lane = wide // 2
    tokens = tok_ref.shape[0]
    blocks = gate.shape[0]
    rows = gate.shape[1]
    ff = gate.shape[2]
    to_view = (1 - v, e, c)
    to_sib = (v, e, y * 2 + 1 - k)
    to_y = (v, e, (1 - y) * 2 + k)

    def remote(src, dst, send, recv, device):
        return pltpu.make_async_remote_copy(
            src_ref=src, dst_ref=dst, send_sem=send, recv_sem=recv,
            device_id=device, device_id_type=pl.DeviceIdType.MESH)

    def expert_at(step):
        return (e + step) % NE

    barrier = pltpu.get_barrier_semaphore()
    others = [to_view, to_sib, to_y] + [(v, expert_at(s), c) for s in range(1, NE)]
    for device in others:
        pl.semaphore_signal(barrier, inc=1, device_id=device, device_id_type=pl.DeviceIdType.MESH)
    pl.semaphore_wait(barrier, len(others))

    send_g = remote(wg_ref, far_g, far_send.at[0], far_recv.at[0], to_view)
    send_u = remote(wu_ref, far_u, far_send.at[1], far_recv.at[1], to_view)
    send_g.start()
    send_u.start()
    send_tok = remote(tok_ref.at[:, pl.ds(pl.multiple_of((1 - k) * half, half), half)], sib_tok,
                      sib_send.at[0], sib_recv.at[0], to_sib)
    send_tok.start()
    send_fake = remote(fake_ref, sib_fake, sib_send.at[1], sib_recv.at[1], to_sib)
    send_fake.start()
    own_g = pltpu.make_async_copy(wg_ref, near_g, near_sem.at[0])
    own_u = pltpu.make_async_copy(wu_ref, near_u, near_sem.at[1])
    own_g.start()
    own_u.start()

    def own_down(j):
        return pltpu.make_async_copy(
            wd_ref.at[:, pl.ds(pl.multiple_of(j * wide, wide), wide)], down.at[j], near_down.at[j])

    def far_down(j):
        return remote(wd_ref.at[:, pl.ds(pl.multiple_of(j * wide, wide), wide)],
                      down.at[per_view + j], down_send.at[j], down_recv.at[j], to_view)

    for j in range(per_view):
        own_down(j).start()

    id0, id1 = ids_ref[0:1, :], ids_ref[1:2, :]
    which = lax.broadcasted_iota(jnp.int32, (16, tokens), 0)
    hits = jnp.where((which == id0) | (which == id1), 1.0, 0.0).astype(BF16)
    earlier = jnp.where(
        lax.broadcasted_iota(jnp.int32, (tokens, tokens), 0)
        < lax.broadcasted_iota(jnp.int32, (tokens, tokens), 1), 1.0, 0.0).astype(BF16)
    before = jnp.dot(hits, earlier, preferred_element_type=F32)
    slot0 = jnp.sum(jnp.where(which == id0, before, 0.0), axis=0, keepdims=True).astype(jnp.int32)
    slot1 = jnp.sum(jnp.where(which == id1, before, 0.0), axis=0, keepdims=True).astype(jnp.int32)
    row = lax.broadcasted_iota(jnp.int32, (NE * PAIR, tokens), 0)
    is0 = row == id0 * PAIR + k * CAP + slot0
    is1 = row == id1 * PAIR + k * CAP + slot1
    code0, code1 = codes_ref[0:1, :], codes_ref[1:2, :]
    hi0, hi1 = (code0 // 32).astype(F32) / 32.0, (code1 // 32).astype(F32) / 32.0
    lo0, lo1 = (code0 % 32).astype(F32) / 1024.0, (code1 % 32).astype(F32) / 1024.0
    hi = jnp.where(is0, hi0, 0.0) + jnp.where(is1, hi1, 0.0)
    lo = jnp.where(is0, lo0, 0.0) + jnp.where(is1, lo1, 0.0)
    place[0] = hi.astype(BF16)
    place[1] = lo.astype(BF16)
    send_place = remote(place, sib_place, sib_send.at[2], sib_recv.at[2], to_sib)
    send_place.start()
    select = jnp.where(is0 | is1, 1.0, 0.0).astype(BF16)
    mine = jnp.dot(select, tok_ref[:, pl.ds(pl.multiple_of(k * half, half), half)],
                   preferred_element_type=F32)
    send_tok.wait_recv()
    send_place.wait_recv()
    sib_hi, sib_lo = sib_place[0].astype(F32), sib_place[1].astype(F32)
    sib_select = jnp.where(sib_hi + sib_lo > 0.0, 1.0, 0.0).astype(BF16)
    both = mine + jnp.dot(sib_select, sib_tok[...], preferred_element_type=F32)
    sent_z[...] = both.astype(BF16).reshape(NE, PAIR, half)
    x[k, y, e] = sent_z[e]

    def z_copy(s):
        peer = expert_at(s)
        return remote(sent_z.at[peer], x.at[k, y, e], z_send.at[s - 1], z_recv.at[s - 1], (v, peer, c))

    def z_arrived(s):
        return remote(sent_z.at[0], x.at[k, y, expert_at(NE - s)], z_send.at[s - 1], z_recv.at[s - 1], to_view)

    def y_copy(s):
        at = x.at[k, y, expert_at(NE - s)]
        return remote(at, at, y_send.at[s], y_recv.at[s], to_y)

    def y_arrived(s):
        at = x.at[k, 1 - y, expert_at(NE - s)]
        return remote(at, at, y_send.at[s], y_recv.at[s], to_y)

    def c_copy(s, far):
        at = x.at[k, (1 - y) if far else y, expert_at(NE - s)]
        return remote(at, at, c_send.at[far, s], c_recv.at[far, s], to_sib)

    def c_arrived(s, far):
        at = x.at[1 - k, (1 - y) if far else y, expert_at(NE - s)]
        return remote(at, at, c_send.at[far, s], c_recv.at[far, s], to_sib)

    for s in range(1, NE):
        z_copy(s).start()
    y_copy(0).start()
    c_copy(0, 0).start()
    combine[0, 0:tokens] = hi.T.astype(BF16)
    combine[1, 0:tokens] = lo.T.astype(BF16)
    combine[0, tokens:2 * tokens] = sib_hi.T.astype(BF16)
    combine[1, tokens:2 * tokens] = sib_lo.T.astype(BF16)
    for s in range(1, NE):
        z_arrived(s).wait_recv()
        y_copy(s).start()
        c_copy(s, 0).start()
    for s in range(NE):
        y_arrived(s).wait_recv()
        c_copy(s, 1).start()
    for far in range(2):
        for s in range(NE):
            c_arrived(s, far).wait_recv()

    def x_rows(view, i):
        return x[view, i // 2, pl.ds((i % 2) * 2, 2)].reshape(rows, half)

    own_g.wait()
    own_u.wait()

    @pl.loop(0, blocks)
    def _(i):
        gate[i] = lax.dot_general(x_rows(v, i), near_g[...], NEAR, preferred_element_type=F32)
        up[i] = lax.dot_general(x_rows(v, i), near_u[...], NEAR, preferred_element_type=F32)

    send_g.wait_recv()

    @pl.loop(0, blocks)
    def _(i):
        gate[i] += lax.dot_general(x_rows(1 - v, i), far_g[...], NEAR, preferred_element_type=F32)

    for j in range(per_view):
        far_down(j).start()
    send_u.wait_recv()

    @pl.loop(0, blocks)
    def _(i):
        u = up[i] + lax.dot_general(x_rows(1 - v, i), far_u[...], NEAR, preferred_element_type=F32)
        g = gate[i]
        hidden[i] = (g / (1.0 + jnp.exp(-g)) * u).astype(BF16)

    def stage_a(j):
        return remote(part.at[j, 1 - k], core_in.at[j], a_send.at[j], a_recv.at[j], to_sib)

    def stage_b(j):
        return remote(pair_sum.at[j, 1 - y], y_in.at[j], b_send.at[j], b_recv.at[j], to_y)

    def stage_c(j, s):
        peer = expert_at(s)
        return remote(y_sum.at[j, peer], back.at[j, e], e_send.at[s - 1, j], e_recv.at[s - 1, j], (v, peer, c))

    def stage_c_in(j, s):
        return remote(y_sum.at[j, 0], back.at[j, expert_at(NE - s)], e_send.at[s - 1, j], e_recv.at[s - 1, j], to_view)

    def stage_d(j):
        return remote(sib_gap.at[j], gap_in.at[j], g_send.at[j], g_recv.at[j], to_sib)

    def columns(j, core):
        first = (j // per_view + v) % 2 * half + (j % per_view) * wide + core * lane
        return pl.ds(pl.multiple_of(first, lane), lane)

    send_fake.wait_recv()

    @pl.loop(0, chunks + 3)
    def _(t):
        @pl.when((t >= 1) & (t < chunks + 1))
        def _():
            j = t - 1
            stage_a(j).wait_recv()
            total = part[j, k].astype(F32) + core_in[j].astype(F32)
            pair_sum[j] = total.astype(BF16).reshape(2, NE * PAIR, lane)
            stage_b(j).start()

        @pl.when((t >= 2) & (t < chunks + 2))
        def _():
            j = t - 2
            stage_b(j).wait_recv()
            total = pair_sum[j, y].astype(F32) + y_in[j].astype(F32)
            y_sum[j] = total.astype(BF16).reshape(NE, PAIR, lane)
            for s in range(1, NE):
                stage_c(j, s).start()
            back[j, e] = y_sum[j, e]

        @pl.when(t >= 3)
        def _():
            j = t - 3
            for s in range(1, NE):
                stage_c_in(j, s).wait_recv()
            result = back[j].reshape(NE * PAIR, lane)
            teacher = jnp.dot(combine[0], result, preferred_element_type=F32) + jnp.dot(
                combine[1], result, preferred_element_type=F32)
            at = columns(j, k)
            sib_gap[j] = (sib_fake[:, at].astype(F32) - teacher[tokens:]).astype(BF16)
            stage_d(j).start()
            out_ref[:, at] = (fake_ref[:, at].astype(F32) - teacher[:tokens]).astype(BF16)

        @pl.when(t < per_view)
        def _():
            own_down(t).wait()

        @pl.when((t >= per_view) & (t < chunks))
        def _():
            far_down(t - per_view).wait_recv()

        @pl.when(t < chunks)
        def _():
            @pl.loop(0, blocks)
            def _(i):
                p = jnp.dot(hidden[i], down[t], preferred_element_type=F32).astype(BF16)
                at = pl.ds(pl.multiple_of(i * rows, rows), rows)
                part[t, 0, at, :] = p[:, :lane]
                part[t, 1, at, :] = p[:, lane:]
            stage_a(t).start()

    @pl.loop(0, chunks)
    def _(j):
        stage_d(j).wait_recv()
        out_ref[:, columns(j, 1 - k)] = gap_in[j]
        stage_a(j).wait_send()
        stage_b(j).wait_send()
        for s in range(1, NE):
            stage_c(j, s).wait_send()
        stage_d(j).wait_send()

    for j in range(per_view):
        far_down(j).wait_send()
    for copy in (send_g, send_u, send_tok, send_fake, send_place):
        copy.wait_send()
    for s in range(1, NE):
        z_copy(s).wait_send()
    for s in range(NE):
        y_copy(s).wait_send()
        c_copy(s, 0).wait_send()
        c_copy(s, 1).wait_send()


def on_device_fused(tokens, expert_ids, gate_codes, fake_score, gate_weight, up_weight, down_weight):
    ff, half = gate_weight.shape[2], gate_weight.shape[1]
    count = tokens.shape[0]
    chunks, wide, lane = 10, 256, 128
    total = 8 * PAIR
    dma = pltpu.SemaphoreType.DMA
    vmem = pl.BlockSpec(memory_space=pltpu.VMEM)
    anywhere = pl.BlockSpec(memory_space=pl.ANY)
    return pl.pallas_call(
        fused,
        out_shape=jax.ShapeDtypeStruct((count, D), BF16),
        in_specs=[vmem] * 4 + [anywhere] * 3,
        out_specs=vmem,
        scratch_shapes=[
            pltpu.VMEM((ff, half), BF16), pltpu.VMEM((ff, half), BF16),
            pltpu.VMEM((ff, half), BF16), pltpu.VMEM((ff, half), BF16),
            pltpu.VMEM((chunks, ff, wide), BF16),
            pltpu.VMEM((2, 2, NE, PAIR, half), BF16),
            pltpu.VMEM((NE, PAIR, half), BF16),
            pltpu.VMEM((4, total // 4, ff), F32), pltpu.VMEM((4, total // 4, ff), F32),
            pltpu.VMEM((4, total // 4, ff), BF16),
            pltpu.VMEM((2, NE * PAIR, count), BF16), pltpu.VMEM((2, NE * PAIR, count), BF16),
            pltpu.VMEM((count, half), BF16), pltpu.VMEM((count, D), BF16),
            pltpu.VMEM((2, 2 * count, NE * PAIR), BF16),
            pltpu.VMEM((chunks, 2, total, lane), BF16),
            pltpu.VMEM((chunks, total, lane), BF16),
            pltpu.VMEM((chunks, 2, NE * PAIR, lane), BF16),
            pltpu.VMEM((chunks, NE * PAIR, lane), BF16),
            pltpu.VMEM((chunks, NE, PAIR, lane), BF16),
            pltpu.VMEM((chunks, NE, PAIR, lane), BF16),
            pltpu.VMEM((chunks, count, lane), BF16), pltpu.VMEM((chunks, count, lane), BF16),
            dma((2,)), dma((2,)), dma((chunks // 2,)), dma((chunks // 2,)), dma((2,)), dma((chunks // 2,)),
            dma((3,)), dma((3,)), dma((NE - 1,)), dma((NE - 1,)), dma((NE,)), dma((NE,)),
            dma((2, NE)), dma((2, NE)),
            dma((chunks,)), dma((chunks,)), dma((chunks,)), dma((chunks,)),
            dma((NE - 1, chunks)), dma((NE - 1, chunks)), dma((chunks,)), dma((chunks,)),
        ],
        compiler_params=pltpu.CompilerParams(
            collective_id=0, has_side_effects=True, vmem_limit_bytes=60 * 1024 * 1024),
        cost_estimate=pl.CostEstimate(
            flops=6 * total * D * ff, bytes_accessed=6 * D * ff, transcendentals=total * ff),
    )(
        expert_ids.T, gate_codes.T, tokens, fake_score,
        gate_weight[0].T, up_weight[0].T, down_weight[0],
    )


def on_device(tokens, expert_ids, gate_codes, fake_score, gate_weight, up_weight, down_weight):
    slots_all = NE * CAP
    hits = expert_ids[:, :, None] == jnp.arange(NE)[None, None, :]
    routed = jnp.sum(hits.astype(jnp.int32), axis=1)
    before = jnp.cumsum(routed, axis=0) - routed
    slot = jnp.sum(jnp.where(hits, before[:, None, :], 0), axis=2)
    target = expert_ids * CAP + slot
    place = target[:, :, None] == jnp.arange(slots_all)[None, None, :]
    select = jnp.any(place, axis=1).astype(jnp.bfloat16)
    outgoing = jnp.dot(select.T, tokens, preferred_element_type=jnp.float32).astype(jnp.bfloat16)
    arrived = lax.all_to_all(
        outgoing.reshape(NE, CAP, D), "expert", split_axis=0, concat_axis=0, tiled=True
    )
    gathered = lax.all_gather(arrived, "col", axis=0, tiled=True)
    inputs = gathered.reshape(-1, D)

    def add_rows(piece):
        return jnp.dot(inputs, piece[0], preferred_element_type=jnp.float32)

    gate = add_rows(lax.all_gather(gate_weight, "view", axis=1, tiled=True))
    up = add_rows(lax.all_gather(up_weight, "view", axis=1, tiled=True))
    hidden = (jax.nn.silu(gate) * up).astype(jnp.bfloat16)
    partial_out = jnp.dot(
        hidden,
        lax.all_gather(down_weight, "view", axis=2, tiled=True)[0],
        preferred_element_type=jnp.float32,
    ).astype(jnp.bfloat16)
    partial_out = lax.optimization_barrier(partial_out).astype(jnp.float32)
    summed = lax.psum_scatter(
        partial_out.astype(jnp.bfloat16), "col", scatter_dimension=0, tiled=True
    )
    back = lax.all_to_all(
        summed.reshape(NE, CAP, D), "expert", split_axis=0, concat_axis=0, tiled=True
    )
    results = back.reshape(slots_all, D)
    weights = gate_codes.astype(jnp.float32) / 1024.0
    teacher = jnp.zeros((tokens.shape[0], D), jnp.float32)
    for route in range(2):
        picker = place[:, route, :].astype(jnp.bfloat16)
        picked = jnp.dot(picker, results, preferred_element_type=jnp.float32)
        teacher = teacher + weights[:, route][:, None] * picked
    return (fake_score.astype(jnp.float32) - teacher).astype(jnp.bfloat16)


def solution(mesh):
    in_specs = (
        P(("view", "expert", "col"), None),
        P(("view", "expert", "col"), None),
        P(("view", "expert", "col"), None),
        P(("view", "expert", "col"), None),
        P("expert", "view", "col"),
        P("expert", "view", "col"),
        P("expert", "col", "view"),
    )
    out_specs = P(("view", "expert", "col"), None)
    return jax.shard_map(
        on_device_fused if mesh.shape["view"] == 2 else on_device, mesh=mesh, in_specs=in_specs, out_specs=out_specs, check_vma=False
    )
```

```python
import functools

import jax
import jax.numpy as jnp
from jax import lax
from jax.experimental import pallas as pl
from jax.experimental.pallas import tpu as pltpu
from jax.sharding import PartitionSpec as P

D = 2560
NE = 4
CAP = 68
PAIR = 144
F32 = jnp.float32
BF16 = jnp.bfloat16
NEAR = (((1,), (1,)), ((), ()))


def fused(ids_ref, codes_ref, tok_ref, fake_ref, wg_ref, wu_ref, wd_ref, out_ref,
          near_g, near_u, far_g, far_u, down, x, sent_z, gate, up, hidden,
          place, sib_place, sib_tok, sib_fake, combine,
          part, core_in, pair_sum, y_in, y_sum, back, sib_gap, gap_in,
          far_send, far_recv, down_send, down_recv, near_sem, near_down,
          sib_send, sib_recv, z_send, z_recv, y_send, y_recv, c_send, c_recv,
          a_send, a_recv, b_send, b_recv, e_send, e_recv, g_send, g_recv):
    v, e, c = lax.axis_index("view"), lax.axis_index("expert"), lax.axis_index("col")
    k, y = c % 2, c // 2
    half = D // 2
    chunks = down.shape[0]
    per_view = chunks // 2
    wide = down.shape[2]
    lane = wide // 2
    tokens = tok_ref.shape[0]
    blocks = gate.shape[0]
    rows = gate.shape[1]
    ff = gate.shape[2]
    to_view = (1 - v, e, c)
    to_sib = (v, e, y * 2 + 1 - k)
    to_y = (v, e, (1 - y) * 2 + k)

    def remote(src, dst, send, recv, device):
        return pltpu.make_async_remote_copy(
            src_ref=src, dst_ref=dst, send_sem=send, recv_sem=recv,
            device_id=device, device_id_type=pl.DeviceIdType.MESH)

    def expert_at(step):
        return (e + step) % NE

    barrier = pltpu.get_barrier_semaphore()
    others = [to_view, to_sib, to_y] + [(v, expert_at(s), c) for s in range(1, NE)]
    for device in others:
        pl.semaphore_signal(barrier, inc=1, device_id=device, device_id_type=pl.DeviceIdType.MESH)
    pl.semaphore_wait(barrier, len(others))

    send_g = remote(wg_ref, far_g, far_send.at[0], far_recv.at[0], to_view)
    send_u = remote(wu_ref, far_u, far_send.at[1], far_recv.at[1], to_view)
    send_g.start()
    send_u.start()
    send_tok = remote(tok_ref.at[:, pl.ds(pl.multiple_of((1 - k) * half, half), half)], sib_tok,
                      sib_send.at[0], sib_recv.at[0], to_sib)
    send_tok.start()
    send_fake = remote(fake_ref, sib_fake, sib_send.at[1], sib_recv.at[1], to_sib)
    send_fake.start()
    own_g = pltpu.make_async_copy(wg_ref, near_g, near_sem.at[0])
    own_u = pltpu.make_async_copy(wu_ref, near_u, near_sem.at[1])
    own_g.start()
    own_u.start()

    def own_down(j):
        return pltpu.make_async_copy(
            wd_ref.at[:, pl.ds(pl.multiple_of(j * wide, wide), wide)], down.at[j], near_down.at[j])

    def far_down(j):
        return remote(wd_ref.at[:, pl.ds(pl.multiple_of(j * wide, wide), wide)],
                      down.at[per_view + j], down_send.at[j], down_recv.at[j], to_view)

    for j in range(per_view):
        own_down(j).start()

    id0, id1 = ids_ref[0:1, :], ids_ref[1:2, :]
    which = lax.broadcasted_iota(jnp.int32, (16, tokens), 0)
    hits = jnp.where((which == id0) | (which == id1), 1.0, 0.0).astype(BF16)
    earlier = jnp.where(
        lax.broadcasted_iota(jnp.int32, (tokens, tokens), 0)
        < lax.broadcasted_iota(jnp.int32, (tokens, tokens), 1), 1.0, 0.0).astype(BF16)
    before = jnp.dot(hits, earlier, preferred_element_type=F32)
    slot0 = jnp.sum(jnp.where(which == id0, before, 0.0), axis=0, keepdims=True).astype(jnp.int32)
    slot1 = jnp.sum(jnp.where(which == id1, before, 0.0), axis=0, keepdims=True).astype(jnp.int32)
    row = lax.broadcasted_iota(jnp.int32, (NE * PAIR, tokens), 0)
    is0 = row == id0 * PAIR + k * CAP + slot0
    is1 = row == id1 * PAIR + k * CAP + slot1
    code0, code1 = codes_ref[0:1, :], codes_ref[1:2, :]
    hi0, hi1 = (code0 // 32).astype(F32) / 32.0, (code1 // 32).astype(F32) / 32.0
    lo0, lo1 = (code0 % 32).astype(F32) / 1024.0, (code1 % 32).astype(F32) / 1024.0
    hi = jnp.where(is0, hi0, 0.0) + jnp.where(is1, hi1, 0.0)
    lo = jnp.where(is0, lo0, 0.0) + jnp.where(is1, lo1, 0.0)
    place[0] = hi.astype(BF16)
    place[1] = lo.astype(BF16)
    send_place = remote(place, sib_place, sib_send.at[2], sib_recv.at[2], to_sib)
    send_place.start()
    select = jnp.where(is0 | is1, 1.0, 0.0).astype(BF16)
    mine = jnp.dot(select, tok_ref[:, pl.ds(pl.multiple_of(k * half, half), half)],
                   preferred_element_type=F32)
    send_tok.wait_recv()
    send_place.wait_recv()
    sib_hi, sib_lo = sib_place[0].astype(F32), sib_place[1].astype(F32)
    sib_select = jnp.where(sib_hi + sib_lo > 0.0, 1.0, 0.0).astype(BF16)
    both = mine + jnp.dot(sib_select, sib_tok[...], preferred_element_type=F32)
    sent_z[...] = both.astype(BF16).reshape(NE, PAIR, half)
    x[k, y, e] = sent_z[e]

    def z_copy(s):
        peer = expert_at(s)
        return remote(sent_z.at[peer], x.at[k, y, e], z_send.at[s - 1], z_recv.at[s - 1], (v, peer, c))

    def z_arrived(s):
        return remote(sent_z.at[0], x.at[k, y, expert_at(NE - s)], z_send.at[s - 1], z_recv.at[s - 1], to_view)

    def y_copy(s):
        at = x.at[k, y, expert_at(NE - s)]
        return remote(at, at, y_send.at[s], y_recv.at[s], to_y)

    def y_arrived(s):
        at = x.at[k, 1 - y, expert_at(NE - s)]
        return remote(at, at, y_send.at[s], y_recv.at[s], to_y)

    def c_copy(s, far):
        at = x.at[k, (1 - y) if far else y, expert_at(NE - s)]
        return remote(at, at, c_send.at[far, s], c_recv.at[far, s], to_sib)

    def c_arrived(s, far):
        at = x.at[1 - k, (1 - y) if far else y, expert_at(NE - s)]
        return remote(at, at, c_send.at[far, s], c_recv.at[far, s], to_sib)

    for s in range(1, NE):
        z_copy(s).start()
    y_copy(0).start()
    c_copy(0, 0).start()
    combine[0, 0:tokens] = hi.T.astype(BF16)
    combine[1, 0:tokens] = lo.T.astype(BF16)
    combine[0, tokens:2 * tokens] = sib_hi.T.astype(BF16)
    combine[1, tokens:2 * tokens] = sib_lo.T.astype(BF16)
    for s in range(1, NE):
        z_arrived(s).wait_recv()
        y_copy(s).start()
        c_copy(s, 0).start()
    for s in range(NE):
        y_arrived(s).wait_recv()
        c_copy(s, 1).start()
    for far in range(2):
        for s in range(NE):
            c_arrived(s, far).wait_recv()

    def x_rows(view, i):
        return x[view, i // 2, pl.ds((i % 2) * 2, 2)].reshape(rows, half)

    own_g.wait()
    own_u.wait()

    @pl.loop(0, blocks)
    def _(i):
        gate[i] = lax.dot_general(x_rows(v, i), near_g[...], NEAR, preferred_element_type=F32)
        up[i] = lax.dot_general(x_rows(v, i), near_u[...], NEAR, preferred_element_type=F32)

    send_g.wait_recv()

    @pl.loop(0, blocks)
    def _(i):
        gate[i] += lax.dot_general(x_rows(1 - v, i), far_g[...], NEAR, preferred_element_type=F32)

    for j in range(per_view):
        far_down(j).start()
    send_u.wait_recv()

    @pl.loop(0, blocks)
    def _(i):
        u = up[i] + lax.dot_general(x_rows(1 - v, i), far_u[...], NEAR, preferred_element_type=F32)
        g = gate[i]
        hidden[i] = (g / (1.0 + jnp.exp(-g)) * u).astype(BF16)

    def block_at(i):
        return pl.ds(pl.multiple_of(i * rows, rows), rows)

    def stage_a(j, i):
        at = block_at(i)
        return remote(part.at[j, 1 - k, at], core_in.at[j, at], a_send.at[i, j], a_recv.at[i, j], to_sib)

    def stage_b(j, piece):
        at = block_at(piece)
        return remote(pair_sum.at[j, 1 - y, at], y_in.at[j, at], b_send.at[piece, j], b_recv.at[piece, j], to_y)

    def stage_c(j, s):
        peer = expert_at(s)
        return remote(y_sum.at[j, peer], back.at[j, e], e_send.at[s - 1, j], e_recv.at[s - 1, j], (v, peer, c))

    def stage_c_in(j, s):
        return remote(y_sum.at[j, 0], back.at[j, expert_at(NE - s)], e_send.at[s - 1, j], e_recv.at[s - 1, j], to_view)

    def stage_d(j):
        return remote(sib_gap.at[j], gap_in.at[j], g_send.at[j], g_recv.at[j], to_sib)

    def columns(j, core):
        first = (j // per_view + v) % 2 * half + (j % per_view) * wide + core * lane
        return pl.ds(pl.multiple_of(first, lane), lane)

    send_fake.wait_recv()

    @pl.loop(0, chunks + 3)
    def _(t):
        @pl.when((t >= 1) & (t < chunks + 1))
        def _():
            j = t - 1

            def add_pair(line, piece):
                stage_a(j, line * 2 + piece).wait_recv()
                at = block_at(line * 2 + piece)
                total = part[j, k, at].astype(F32) + core_in[j, at].astype(F32)
                pair_sum[j, line, block_at(piece)] = total.astype(BF16)

            for piece in range(2):
                add_pair(1 - y, piece)
                stage_b(j, piece).start()
            for piece in range(2):
                add_pair(y, piece)

        @pl.when((t >= 2) & (t < chunks + 2))
        def _():
            j = t - 2
            for piece in range(2):
                stage_b(j, piece).wait_recv()
                at = block_at(piece)
                total = pair_sum[j, y, at].astype(F32) + y_in[j, at].astype(F32)
                y_sum[j, 2 * piece:2 * piece + 2] = total.astype(BF16).reshape(2, PAIR, lane)
                for peer in (2 * piece, 2 * piece + 1):
                    @pl.when(peer != e)
                    def _():
                        stage_c(j, (peer - e + NE) % NE).start()
            back[j, e] = y_sum[j, e]

        @pl.when(t >= 3)
        def _():
            j = t - 3
            for s in range(1, NE):
                stage_c_in(j, s).wait_recv()
            result = back[j].reshape(NE * PAIR, lane)
            at = columns(j, k)

            def teacher(first):
                return jnp.dot(combine[0, first:first + tokens], result, preferred_element_type=F32) + jnp.dot(
                    combine[1, first:first + tokens], result, preferred_element_type=F32)

            sib_gap[j] = (sib_fake[:, at].astype(F32) - teacher(tokens)).astype(BF16)
            stage_d(j).start()
            out_ref[:, at] = (fake_ref[:, at].astype(F32) - teacher(0)).astype(BF16)

        @pl.when(t < per_view)
        def _():
            own_down(t).wait()

        @pl.when((t >= per_view) & (t < chunks))
        def _():
            far_down(t - per_view).wait_recv()

        @pl.when(t < chunks)
        def _():
            @pl.loop(0, blocks)
            def _(turn):
                i = ((turn + 1 + y) % 2) * 2 + turn // 2
                p = jnp.dot(hidden[i], down[t], preferred_element_type=F32).astype(BF16)
                at = pl.ds(pl.multiple_of(i * rows, rows), rows)
                part[t, 0, at, :] = p[:, :lane]
                part[t, 1, at, :] = p[:, lane:]
                stage_a(t, i).start()

    @pl.loop(0, chunks)
    def _(j):
        stage_d(j).wait_recv()
        out_ref[:, columns(j, 1 - k)] = gap_in[j]
        for i in range(blocks):
            stage_a(j, i).wait_send()
        for piece in range(2):
            stage_b(j, piece).wait_send()
        for s in range(1, NE):
            stage_c(j, s).wait_send()
        stage_d(j).wait_send()

    for j in range(per_view):
        far_down(j).wait_send()
    for copy in (send_g, send_u, send_tok, send_fake, send_place):
        copy.wait_send()
    for s in range(1, NE):
        z_copy(s).wait_send()
    for s in range(NE):
        y_copy(s).wait_send()
        c_copy(s, 0).wait_send()
        c_copy(s, 1).wait_send()


def on_device_fused(tokens, expert_ids, gate_codes, fake_score, gate_weight, up_weight, down_weight):
    ff, half = gate_weight.shape[2], gate_weight.shape[1]
    count = tokens.shape[0]
    chunks, wide, lane = 10, 256, 128
    total = 8 * PAIR
    dma = pltpu.SemaphoreType.DMA
    vmem = pl.BlockSpec(memory_space=pltpu.VMEM)
    anywhere = pl.BlockSpec(memory_space=pl.ANY)
    return pl.pallas_call(
        fused,
        out_shape=jax.ShapeDtypeStruct((count, D), BF16),
        in_specs=[vmem] * 4 + [anywhere] * 3,
        out_specs=vmem,
        scratch_shapes=[
            pltpu.VMEM((ff, half), BF16), pltpu.VMEM((ff, half), BF16),
            pltpu.VMEM((ff, half), BF16), pltpu.VMEM((ff, half), BF16),
            pltpu.VMEM((chunks, ff, wide), BF16),
            pltpu.VMEM((2, 2, NE, PAIR, half), BF16),
            pltpu.VMEM((NE, PAIR, half), BF16),
            pltpu.VMEM((4, total // 4, ff), F32), pltpu.VMEM((4, total // 4, ff), F32),
            pltpu.VMEM((4, total // 4, ff), BF16),
            pltpu.VMEM((2, NE * PAIR, count), BF16), pltpu.VMEM((2, NE * PAIR, count), BF16),
            pltpu.VMEM((count, half), BF16), pltpu.VMEM((count, D), BF16),
            pltpu.VMEM((2, 2 * count, NE * PAIR), BF16),
            pltpu.VMEM((chunks, 2, total, lane), BF16),
            pltpu.VMEM((chunks, total, lane), BF16),
            pltpu.VMEM((chunks, 2, NE * PAIR, lane), BF16),
            pltpu.VMEM((chunks, NE * PAIR, lane), BF16),
            pltpu.VMEM((chunks, NE, PAIR, lane), BF16),
            pltpu.VMEM((chunks, NE, PAIR, lane), BF16),
            pltpu.VMEM((chunks, count, lane), BF16), pltpu.VMEM((chunks, count, lane), BF16),
            dma((2,)), dma((2,)), dma((chunks // 2,)), dma((chunks // 2,)), dma((2,)), dma((chunks // 2,)),
            dma((3,)), dma((3,)), dma((NE - 1,)), dma((NE - 1,)), dma((NE,)), dma((NE,)),
            dma((2, NE)), dma((2, NE)),
            dma((4, chunks)), dma((4, chunks)), dma((2, chunks)), dma((2, chunks)),
            dma((NE - 1, chunks)), dma((NE - 1, chunks)), dma((chunks,)), dma((chunks,)),
        ],
        compiler_params=pltpu.CompilerParams(
            collective_id=0, has_side_effects=True, vmem_limit_bytes=57 * 1024 * 1024),
        cost_estimate=pl.CostEstimate(
            flops=6 * total * D * ff, bytes_accessed=6 * D * ff, transcendentals=total * ff),
    )(
        expert_ids.T, gate_codes.T, tokens, fake_score,
        gate_weight[0].T, up_weight[0].T, down_weight[0],
    )


def on_device(tokens, expert_ids, gate_codes, fake_score, gate_weight, up_weight, down_weight):
    slots_all = NE * CAP
    hits = expert_ids[:, :, None] == jnp.arange(NE)[None, None, :]
    routed = jnp.sum(hits.astype(jnp.int32), axis=1)
    before = jnp.cumsum(routed, axis=0) - routed
    slot = jnp.sum(jnp.where(hits, before[:, None, :], 0), axis=2)
    target = expert_ids * CAP + slot
    place = target[:, :, None] == jnp.arange(slots_all)[None, None, :]
    select = jnp.any(place, axis=1).astype(jnp.bfloat16)
    outgoing = jnp.dot(select.T, tokens, preferred_element_type=jnp.float32).astype(jnp.bfloat16)
    arrived = lax.all_to_all(
        outgoing.reshape(NE, CAP, D), "expert", split_axis=0, concat_axis=0, tiled=True
    )
    gathered = lax.all_gather(arrived, "col", axis=0, tiled=True)
    inputs = gathered.reshape(-1, D)

    def add_rows(piece):
        return jnp.dot(inputs, piece[0], preferred_element_type=jnp.float32)

    gate = add_rows(lax.all_gather(gate_weight, "view", axis=1, tiled=True))
    up = add_rows(lax.all_gather(up_weight, "view", axis=1, tiled=True))
    hidden = (jax.nn.silu(gate) * up).astype(jnp.bfloat16)
    partial_out = jnp.dot(
        hidden,
        lax.all_gather(down_weight, "view", axis=2, tiled=True)[0],
        preferred_element_type=jnp.float32,
    ).astype(jnp.bfloat16)
    partial_out = lax.optimization_barrier(partial_out).astype(jnp.float32)
    summed = lax.psum_scatter(
        partial_out.astype(jnp.bfloat16), "col", scatter_dimension=0, tiled=True
    )
    back = lax.all_to_all(
        summed.reshape(NE, CAP, D), "expert", split_axis=0, concat_axis=0, tiled=True
    )
    results = back.reshape(slots_all, D)
    weights = gate_codes.astype(jnp.float32) / 1024.0
    teacher = jnp.zeros((tokens.shape[0], D), jnp.float32)
    for route in range(2):
        picker = place[:, route, :].astype(jnp.bfloat16)
        picked = jnp.dot(picker, results, preferred_element_type=jnp.float32)
        teacher = teacher + weights[:, route][:, None] * picked
    return (fake_score.astype(jnp.float32) - teacher).astype(jnp.bfloat16)


def solution(mesh):
    in_specs = (
        P(("view", "expert", "col"), None),
        P(("view", "expert", "col"), None),
        P(("view", "expert", "col"), None),
        P(("view", "expert", "col"), None),
        P("expert", "view", "col"),
        P("expert", "view", "col"),
        P("expert", "col", "view"),
    )
    out_specs = P(("view", "expert", "col"), None)
    return jax.shard_map(
        on_device_fused if mesh.shape["view"] == 2 else on_device, mesh=mesh, in_specs=in_specs, out_specs=out_specs, check_vma=False
    )
```

```python
import functools

import jax
import jax.numpy as jnp
from jax import lax
from jax.experimental import pallas as pl
from jax.experimental.pallas import tpu as pltpu
from jax.sharding import PartitionSpec as P

D = 2560
NE = 4
CAP = 68
PAIR = 144
F32 = jnp.float32
BF16 = jnp.bfloat16
NEAR = (((1,), (1,)), ((), ()))


def fused(ids_ref, codes_ref, tok_ref, wg_ref, wu_ref, wd_ref, out_ref,
          near_g, near_u, far_g, far_u, down, x, sent_z, gate, up, hidden,
          place, sib_place, sib_tok, combine,
          part, core_in, pair_sum, y_in, y_sum, back, sib_gap, gap_in,
          far_send, far_recv, down_send, down_recv, near_sem, near_down,
          sib_send, sib_recv, z_send, z_recv, y_send, y_recv, c_send, c_recv,
          a_send, a_recv, b_send, b_recv, e_send, e_recv, g_send, g_recv):
    v, e, c = lax.axis_index("view"), lax.axis_index("expert"), lax.axis_index("col")
    k, y = c % 2, c // 2
    half = D // 2
    chunks = down.shape[0]
    per_view = chunks // 2
    wide = down.shape[2]
    lane = wide // 2
    tokens = tok_ref.shape[0]
    blocks = gate.shape[0]
    rows = gate.shape[1]
    ff = gate.shape[2]
    to_view = (1 - v, e, c)
    to_sib = (v, e, y * 2 + 1 - k)
    to_y = (v, e, (1 - y) * 2 + k)

    def remote(src, dst, send, recv, device):
        return pltpu.make_async_remote_copy(
            src_ref=src, dst_ref=dst, send_sem=send, recv_sem=recv,
            device_id=device, device_id_type=pl.DeviceIdType.MESH)

    def expert_at(step):
        return (e + step) % NE

    barrier = pltpu.get_barrier_semaphore()
    others = [to_view, to_sib, to_y] + [(v, expert_at(s), c) for s in range(1, NE)]
    for device in others:
        pl.semaphore_signal(barrier, inc=1, device_id=device, device_id_type=pl.DeviceIdType.MESH)
    pl.semaphore_wait(barrier, len(others))

    send_g = remote(wg_ref, far_g, far_send.at[0], far_recv.at[0], to_view)
    send_u = remote(wu_ref, far_u, far_send.at[1], far_recv.at[1], to_view)
    send_g.start()
    send_u.start()
    send_tok = remote(tok_ref.at[:, pl.ds(pl.multiple_of((1 - k) * half, half), half)], sib_tok,
                      sib_send.at[0], sib_recv.at[0], to_sib)
    send_tok.start()
    own_g = pltpu.make_async_copy(wg_ref, near_g, near_sem.at[0])
    own_u = pltpu.make_async_copy(wu_ref, near_u, near_sem.at[1])
    own_g.start()
    own_u.start()

    def own_down(j):
        return pltpu.make_async_copy(
            wd_ref.at[:, pl.ds(pl.multiple_of(j * wide, wide), wide)], down.at[j], near_down.at[j])

    def far_down(j):
        return remote(wd_ref.at[:, pl.ds(pl.multiple_of(j * wide, wide), wide)],
                      down.at[per_view + j], down_send.at[j], down_recv.at[j], to_view)

    for j in range(per_view):
        own_down(j).start()

    id0, id1 = ids_ref[0:1, :], ids_ref[1:2, :]
    which = lax.broadcasted_iota(jnp.int32, (16, tokens), 0)
    hits = jnp.where((which == id0) | (which == id1), 1.0, 0.0).astype(BF16)
    earlier = jnp.where(
        lax.broadcasted_iota(jnp.int32, (tokens, tokens), 0)
        < lax.broadcasted_iota(jnp.int32, (tokens, tokens), 1), 1.0, 0.0).astype(BF16)
    before = jnp.dot(hits, earlier, preferred_element_type=F32)
    slot0 = jnp.sum(jnp.where(which == id0, before, 0.0), axis=0, keepdims=True).astype(jnp.int32)
    slot1 = jnp.sum(jnp.where(which == id1, before, 0.0), axis=0, keepdims=True).astype(jnp.int32)
    row = lax.broadcasted_iota(jnp.int32, (NE * PAIR, tokens), 0)
    is0 = row == id0 * PAIR + k * CAP + slot0
    is1 = row == id1 * PAIR + k * CAP + slot1
    code0, code1 = codes_ref[0:1, :], codes_ref[1:2, :]
    hi0, hi1 = (code0 // 32).astype(F32) / 32.0, (code1 // 32).astype(F32) / 32.0
    lo0, lo1 = (code0 % 32).astype(F32) / 1024.0, (code1 % 32).astype(F32) / 1024.0
    hi = jnp.where(is0, hi0, 0.0) + jnp.where(is1, hi1, 0.0)
    lo = jnp.where(is0, lo0, 0.0) + jnp.where(is1, lo1, 0.0)
    place[0] = hi.astype(BF16)
    place[1] = lo.astype(BF16)
    send_place = remote(place, sib_place, sib_send.at[2], sib_recv.at[2], to_sib)
    send_place.start()
    select = jnp.where(is0 | is1, 1.0, 0.0).astype(BF16)
    mine = jnp.dot(select, tok_ref[:, pl.ds(pl.multiple_of(k * half, half), half)],
                   preferred_element_type=F32)
    send_tok.wait_recv()
    send_place.wait_recv()
    sib_hi, sib_lo = sib_place[0].astype(F32), sib_place[1].astype(F32)
    sib_select = jnp.where(sib_hi + sib_lo > 0.0, 1.0, 0.0).astype(BF16)
    both = mine + jnp.dot(sib_select, sib_tok[...], preferred_element_type=F32)
    sent_z[...] = both.astype(BF16).reshape(NE, PAIR, half)
    x[k, y, e] = sent_z[e]

    def z_copy(s):
        peer = expert_at(s)
        return remote(sent_z.at[peer], x.at[k, y, e], z_send.at[s - 1], z_recv.at[s - 1], (v, peer, c))

    def z_arrived(s):
        return remote(sent_z.at[0], x.at[k, y, expert_at(NE - s)], z_send.at[s - 1], z_recv.at[s - 1], to_view)

    def y_copy(s):
        at = x.at[k, y, expert_at(NE - s)]
        return remote(at, at, y_send.at[s], y_recv.at[s], to_y)

    def y_arrived(s):
        at = x.at[k, 1 - y, expert_at(NE - s)]
        return remote(at, at, y_send.at[s], y_recv.at[s], to_y)

    def c_copy(s, far):
        at = x.at[k, (1 - y) if far else y, expert_at(NE - s)]
        return remote(at, at, c_send.at[far, s], c_recv.at[far, s], to_sib)

    def c_arrived(s, far):
        at = x.at[1 - k, (1 - y) if far else y, expert_at(NE - s)]
        return remote(at, at, c_send.at[far, s], c_recv.at[far, s], to_sib)

    for s in range(1, NE):
        z_copy(s).start()
    y_copy(0).start()
    c_copy(0, 0).start()
    combine[0, 0:tokens] = hi.T.astype(BF16)
    combine[1, 0:tokens] = lo.T.astype(BF16)
    combine[0, tokens:2 * tokens] = sib_hi.T.astype(BF16)
    combine[1, tokens:2 * tokens] = sib_lo.T.astype(BF16)
    for s in range(1, NE):
        z_arrived(s).wait_recv()
        y_copy(s).start()
        c_copy(s, 0).start()
    for s in range(NE):
        y_arrived(s).wait_recv()
        c_copy(s, 1).start()
    for far in range(2):
        for s in range(NE):
            c_arrived(s, far).wait_recv()

    def x_rows(view, i):
        return x[view, i // 2, pl.ds((i % 2) * 2, 2)].reshape(rows, half)

    own_g.wait()
    own_u.wait()

    @pl.loop(0, blocks)
    def _(i):
        gate[i] = lax.dot_general(x_rows(v, i), near_g[...], NEAR, preferred_element_type=F32)
        up[i] = lax.dot_general(x_rows(v, i), near_u[...], NEAR, preferred_element_type=F32)

    send_g.wait_recv()

    @pl.loop(0, blocks)
    def _(i):
        gate[i] += lax.dot_general(x_rows(1 - v, i), far_g[...], NEAR, preferred_element_type=F32)

    for j in range(per_view):
        far_down(j).start()
    send_u.wait_recv()

    @pl.loop(0, blocks)
    def _(i):
        u = up[i] + lax.dot_general(x_rows(1 - v, i), far_u[...], NEAR, preferred_element_type=F32)
        g = gate[i]
        hidden[i] = (g / (1.0 + jnp.exp(-g)) * u).astype(BF16)

    def block_at(i):
        return pl.ds(pl.multiple_of(i * rows, rows), rows)

    def stage_a(j, i):
        at = block_at(i)
        return remote(part.at[j, 1 - k, at], core_in.at[j, at], a_send.at[i, j], a_recv.at[i, j], to_sib)

    def stage_b(j, piece):
        at = block_at(piece)
        return remote(pair_sum.at[j, 1 - y, at], y_in.at[j, at], b_send.at[piece, j], b_recv.at[piece, j], to_y)

    def stage_c(j, s):
        peer = expert_at(s)
        return remote(y_sum.at[j, peer], back.at[j, e], e_send.at[s - 1, j], e_recv.at[s - 1, j], (v, peer, c))

    def stage_c_in(j, s):
        return remote(y_sum.at[j, 0], back.at[j, expert_at(NE - s)], e_send.at[s - 1, j], e_recv.at[s - 1, j], to_view)

    def stage_d(j):
        return remote(sib_gap.at[j], gap_in.at[j], g_send.at[j], g_recv.at[j], to_sib)

    def columns(j, core):
        first = (j // per_view + v) % 2 * half + (j % per_view) * wide + core * lane
        return pl.ds(pl.multiple_of(first, lane), lane)

    @pl.loop(0, chunks + 3)
    def _(t):
        @pl.when((t >= 1) & (t < chunks + 1))
        def _():
            j = t - 1

            def add_pair(line, piece):
                stage_a(j, line * 2 + piece).wait_recv()
                at = block_at(line * 2 + piece)
                total = part[j, k, at].astype(F32) + core_in[j, at].astype(F32)
                pair_sum[j, line, block_at(piece)] = total.astype(BF16)

            for piece in range(2):
                add_pair(1 - y, piece)
                stage_b(j, piece).start()
            for piece in range(2):
                add_pair(y, piece)

        @pl.when((t >= 2) & (t < chunks + 2))
        def _():
            j = t - 2
            for piece in range(2):
                stage_b(j, piece).wait_recv()
                at = block_at(piece)
                total = pair_sum[j, y, at].astype(F32) + y_in[j, at].astype(F32)
                y_sum[j, 2 * piece:2 * piece + 2] = total.astype(BF16).reshape(2, PAIR, lane)
                for peer in (2 * piece, 2 * piece + 1):
                    @pl.when(peer != e)
                    def _():
                        stage_c(j, (peer - e + NE) % NE).start()
            back[j, e] = y_sum[j, e]

        @pl.when(t >= 3)
        def _():
            j = t - 3
            for s in range(1, NE):
                stage_c_in(j, s).wait_recv()
            result = back[j].reshape(NE * PAIR, lane)
            at = columns(j, k)

            def teacher(first):
                return jnp.dot(combine[0, first:first + tokens], result, preferred_element_type=F32) + jnp.dot(
                    combine[1, first:first + tokens], result, preferred_element_type=F32)

            sib_gap[j] = teacher(tokens)
            stage_d(j).start()
            out_ref[:, at] = teacher(0)

        @pl.when(t < per_view)
        def _():
            own_down(t).wait()

        @pl.when((t >= per_view) & (t < chunks))
        def _():
            far_down(t - per_view).wait_recv()

        @pl.when(t < chunks)
        def _():
            @pl.loop(0, blocks)
            def _(turn):
                i = ((turn + 1 + y) % 2) * 2 + turn // 2
                p = jnp.dot(hidden[i], down[t], preferred_element_type=F32).astype(BF16)
                at = pl.ds(pl.multiple_of(i * rows, rows), rows)
                part[t, 0, at, :] = p[:, :lane]
                part[t, 1, at, :] = p[:, lane:]
                stage_a(t, i).start()

    @pl.loop(0, chunks)
    def _(j):
        stage_d(j).wait_recv()
        out_ref[:, columns(j, 1 - k)] = gap_in[j]
        for i in range(blocks):
            stage_a(j, i).wait_send()
        for piece in range(2):
            stage_b(j, piece).wait_send()
        for s in range(1, NE):
            stage_c(j, s).wait_send()
        stage_d(j).wait_send()

    for j in range(per_view):
        far_down(j).wait_send()
    for copy in (send_g, send_u, send_tok, send_place):
        copy.wait_send()
    for s in range(1, NE):
        z_copy(s).wait_send()
    for s in range(NE):
        y_copy(s).wait_send()
        c_copy(s, 0).wait_send()
        c_copy(s, 1).wait_send()


def on_device_fused(tokens, expert_ids, gate_codes, fake_score, gate_weight, up_weight, down_weight):
    ff, half = gate_weight.shape[2], gate_weight.shape[1]
    count = tokens.shape[0]
    chunks, wide, lane = 10, 256, 128
    total = 8 * PAIR
    dma = pltpu.SemaphoreType.DMA
    vmem = pl.BlockSpec(memory_space=pltpu.VMEM)
    anywhere = pl.BlockSpec(memory_space=pl.ANY)
    teacher = pl.pallas_call(
        fused,
        out_shape=jax.ShapeDtypeStruct((count, D), F32),
        in_specs=[vmem] * 3 + [anywhere] * 3,
        out_specs=vmem,
        scratch_shapes=[
            pltpu.VMEM((ff, half), BF16), pltpu.VMEM((ff, half), BF16),
            pltpu.VMEM((ff, half), BF16), pltpu.VMEM((ff, half), BF16),
            pltpu.VMEM((chunks, ff, wide), BF16),
            pltpu.VMEM((2, 2, NE, PAIR, half), BF16),
            pltpu.VMEM((NE, PAIR, half), BF16),
            pltpu.VMEM((4, total // 4, ff), F32), pltpu.VMEM((4, total // 4, ff), F32),
            pltpu.VMEM((4, total // 4, ff), BF16),
            pltpu.VMEM((2, NE * PAIR, count), BF16), pltpu.VMEM((2, NE * PAIR, count), BF16),
            pltpu.VMEM((count, half), BF16),
            pltpu.VMEM((2, 2 * count, NE * PAIR), BF16),
            pltpu.VMEM((chunks, 2, total, lane), BF16),
            pltpu.VMEM((chunks, total, lane), BF16),
            pltpu.VMEM((chunks, 2, NE * PAIR, lane), BF16),
            pltpu.VMEM((chunks, NE * PAIR, lane), BF16),
            pltpu.VMEM((chunks, NE, PAIR, lane), BF16),
            pltpu.VMEM((chunks, NE, PAIR, lane), BF16),
            pltpu.VMEM((chunks, count, lane), F32), pltpu.VMEM((chunks, count, lane), F32),
            dma((2,)), dma((2,)), dma((chunks // 2,)), dma((chunks // 2,)), dma((2,)), dma((chunks // 2,)),
            dma((3,)), dma((3,)), dma((NE - 1,)), dma((NE - 1,)), dma((NE,)), dma((NE,)),
            dma((2, NE)), dma((2, NE)),
            dma((4, chunks)), dma((4, chunks)), dma((2, chunks)), dma((2, chunks)),
            dma((NE - 1, chunks)), dma((NE - 1, chunks)), dma((chunks,)), dma((chunks,)),
        ],
        compiler_params=pltpu.CompilerParams(
            collective_id=0, has_side_effects=True, vmem_limit_bytes=57 * 1024 * 1024),
        cost_estimate=pl.CostEstimate(
            flops=6 * total * D * ff, bytes_accessed=6 * D * ff, transcendentals=total * ff),
    )(
        expert_ids.T, gate_codes.T, tokens,
        gate_weight[0].T, up_weight[0].T, down_weight[0],
    )
    return (fake_score.astype(F32) - teacher).astype(BF16)


def on_device(tokens, expert_ids, gate_codes, fake_score, gate_weight, up_weight, down_weight):
    slots_all = NE * CAP
    hits = expert_ids[:, :, None] == jnp.arange(NE)[None, None, :]
    routed = jnp.sum(hits.astype(jnp.int32), axis=1)
    before = jnp.cumsum(routed, axis=0) - routed
    slot = jnp.sum(jnp.where(hits, before[:, None, :], 0), axis=2)
    target = expert_ids * CAP + slot
    place = target[:, :, None] == jnp.arange(slots_all)[None, None, :]
    select = jnp.any(place, axis=1).astype(jnp.bfloat16)
    outgoing = jnp.dot(select.T, tokens, preferred_element_type=jnp.float32).astype(jnp.bfloat16)
    arrived = lax.all_to_all(
        outgoing.reshape(NE, CAP, D), "expert", split_axis=0, concat_axis=0, tiled=True
    )
    gathered = lax.all_gather(arrived, "col", axis=0, tiled=True)
    inputs = gathered.reshape(-1, D)

    def add_rows(piece):
        return jnp.dot(inputs, piece[0], preferred_element_type=jnp.float32)

    gate = add_rows(lax.all_gather(gate_weight, "view", axis=1, tiled=True))
    up = add_rows(lax.all_gather(up_weight, "view", axis=1, tiled=True))
    hidden = (jax.nn.silu(gate) * up).astype(jnp.bfloat16)
    partial_out = jnp.dot(
        hidden,
        lax.all_gather(down_weight, "view", axis=2, tiled=True)[0],
        preferred_element_type=jnp.float32,
    ).astype(jnp.bfloat16)
    partial_out = lax.optimization_barrier(partial_out).astype(jnp.float32)
    summed = lax.psum_scatter(
        partial_out.astype(jnp.bfloat16), "col", scatter_dimension=0, tiled=True
    )
    back = lax.all_to_all(
        summed.reshape(NE, CAP, D), "expert", split_axis=0, concat_axis=0, tiled=True
    )
    results = back.reshape(slots_all, D)
    weights = gate_codes.astype(jnp.float32) / 1024.0
    teacher = jnp.zeros((tokens.shape[0], D), jnp.float32)
    for route in range(2):
        picker = place[:, route, :].astype(jnp.bfloat16)
        picked = jnp.dot(picker, results, preferred_element_type=jnp.float32)
        teacher = teacher + weights[:, route][:, None] * picked
    return (fake_score.astype(jnp.float32) - teacher).astype(jnp.bfloat16)


def solution(mesh):
    in_specs = (
        P(("view", "expert", "col"), None),
        P(("view", "expert", "col"), None),
        P(("view", "expert", "col"), None),
        P(("view", "expert", "col"), None),
        P("expert", "view", "col"),
        P("expert", "view", "col"),
        P("expert", "col", "view"),
    )
    out_specs = P(("view", "expert", "col"), None)
    return jax.shard_map(
        on_device_fused if mesh.shape["view"] == 2 else on_device, mesh=mesh, in_specs=in_specs, out_specs=out_specs, check_vma=False
    )
```
